32 devices in a mesh: vec: 16 (over z, y, x), orb: 2 (over core).
Axes of the slice: x: 2, y: 2, z: 4, core: 2. Of those that a mesh axis runs over, the one named last changes fastest.
Arguments:
- cholesky: bfloat16 [64, 2048, 2048], P('vec', 'orb'), may hold values from -4 to 4
- active_coeff: bfloat16 [2048, 24], replicated, may hold values from -0.125 to 0.125
- pair_density: bfloat16 [24, 24, 576], replicated, may hold values from -0.0546875 to 0.0546875
Outputs:
- active_integrals: float32 [2048, 24, 576], P(('orb', 'vec'))
- general_fock: float32 [2048, 24], P(('orb', 'vec'))
The draws below stay inside these ranges and needn't reach their ends.
All inputs are finite; a program needn't handle non-finite values.
Results may differ from the reference program's by a relative error of at most 0.0049.
Values may be sent and summed in bfloat16 or wider, within the bound.
No kernel may reach another device: no remote copies, remote signals or barrier semaphores. Data moves between devices by JAX's collectives and lax.ppermute only.
A program may use at most 64 MiB of HBM per device.

```python
import jax
import jax.numpy as jnp
from jax import lax

NB = 2048
NA = 24
NQ = 64


def block_scale(own_key, shape, pieces, least, largest):
    factor_of = 1.0
    for axis_at, parts in pieces:
        draws = jax.random.uniform(jax.random.fold_in(jax.random.fold_in(own_key, 6), axis_at), (parts,), jnp.float32, least / len(pieces), largest / len(pieces))
        factor_of = factor_of * jnp.repeat(jnp.exp(draws), shape[axis_at] // parts).reshape((-1,) + (1,) * (len(shape) - 1 - axis_at))
    return factor_of


def bell_draw(key, shape, width, most, pieces=(), dtype=jnp.bfloat16):
    array = width * jax.random.normal(key, shape, jnp.float32)
    if pieces:
        array = array * block_scale(key, shape, pieces, -0.22, 0.18)
    return jnp.clip(array, -most, most).astype(dtype)


def setup_inputs(seed: int = 0) -> dict:
    key_of = jax.random.split(jax.random.key(seed), 4)
    cholesky = bell_draw(key_of[0], (NQ, NB, NB), 0.25, 4.0, ((0, 16), (1, 2)))
    active_coeff = bell_draw(key_of[1], (NB, NA), NB ** -0.5, 0.125)
    pair_density = bell_draw(key_of[2], (NA, NA, NA * NA), (NA * NA * NA) ** -0.5, 0.0546875)
    return {"cholesky": cholesky, "active_coeff": active_coeff, "pair_density": pair_density}


def reference(cholesky, active_coeff, pair_density):
    coeff_wide = active_coeff.astype(jnp.float32)

    def transform(vector):
        return jnp.dot(vector.astype(jnp.float32), coeff_wide, precision=lax.Precision.HIGHEST)

    half = lax.map(transform, cholesky).astype(jnp.bfloat16)
    half_wide = half.astype(jnp.float32)
    active_sum = jnp.einsum("mv,qmw->qvw", coeff_wide, half_wide, precision=lax.Precision.HIGHEST)
    active = active_sum.reshape(NQ, NA * NA).astype(jnp.bfloat16)
    active_wide = active.astype(jnp.float32)
    integrals = jnp.einsum("qmu,qx->mux", half_wide, active_wide, precision=lax.Precision.HIGHEST)
    density = pair_density.astype(jnp.float32).reshape(NA, NA * NA * NA)
    fock = jnp.dot(integrals.reshape(NB, NA * NA * NA), density.T, precision=lax.Precision.HIGHEST)
    return integrals, fock
```

```python
import functools

import jax
import jax.numpy as jnp
from jax import lax
from jax.experimental import pallas as pl
from jax.experimental.pallas import tpu as pltpu
from jax.sharding import PartitionSpec as P

LANES = 128
SUBLANES = 8
BF16 = jnp.bfloat16
F32 = jnp.float32


def transform_kernel(orb_ref, chol_ref, coeff_hbm, half_ref, partial_ref, rows_buf, coeff_row, sems, coeff_sem):
    n_act = coeff_hbm.shape[0]
    rows_all = chol_ref.shape[0]
    block_rows = half_ref.shape[0] * LANES
    size = block_rows // 2
    small = size // 2
    bigs = rows_all // size

    def copy(start, count, sem):
        rows = pl.ds(start, count)
        return pltpu.make_async_copy(chol_ref.at[rows], rows_buf.at[rows], sem)

    def small_copy(i):
        return copy(pl.multiple_of(i * small, small), small, sems.at[i])

    def big_copy(i):
        return copy(pl.multiple_of(i * size, size), size, sems.at[i + 1])

    def step(start, count):
        value = lax.dot_general(
            coeff_row[...],
            rows_buf[pl.ds(start, count), :],
            (((1,), (1,)), ((), ())),
            preferred_element_type=F32,
        )
        rows = pl.ds(pl.multiple_of(lax.div(start, block_rows) * n_act, n_act), n_act)
        tile = lax.div(lax.rem(start, block_rows), LANES)
        value = value.astype(BF16).astype(F32)
        for i in range(count // LANES):
            half_ref[tile + i, rows, :] = value[:, i * LANES:(i + 1) * LANES]

    coeff_copy = pltpu.make_async_copy(coeff_hbm, coeff_row, coeff_sem)
    coeff_copy.start()

    @pl.loop(0, 2)
    def _(i):
        small_copy(i).start()

    @pl.loop(1, bigs)
    def _(i):
        big_copy(i).start()

    coeff_copy.wait()

    @pl.loop(0, 2)
    def _(i):
        small_copy(i).wait()
        step(pl.multiple_of(i * small, small), small)

    @pl.loop(1, bigs)
    def _(i):
        big_copy(i).wait()
        step(pl.multiple_of(i * size, size), size)

    own = pl.multiple_of(orb_ref[0] * block_rows, block_rows)
    partial_ref[...] = lax.dot_general(
        coeff_row[:, pl.ds(own, block_rows)],
        jnp.concatenate([half_ref[i] for i in range(half_ref.shape[0])], axis=1).astype(BF16),
        (((1,), (1,)), ((), ())),
        preferred_element_type=F32,
    )


def transform(cholesky, coeff_t, orb_pos):
    vecs, block_rows, basis = cholesky.shape
    n_act = coeff_t.shape[0]
    width = vecs * n_act
    flat = cholesky.reshape(vecs * block_rows, basis)
    return pl.pallas_call(
        transform_kernel,
        out_shape=(
            jax.ShapeDtypeStruct((block_rows // LANES, width, LANES), F32),
            jax.ShapeDtypeStruct((n_act, width), F32),
        ),
        in_specs=[
            pl.BlockSpec(memory_space=pltpu.SMEM),
            pl.BlockSpec(memory_space=pltpu.HBM),
            pl.BlockSpec(memory_space=pltpu.HBM),
        ],
        out_specs=(pl.BlockSpec(memory_space=pltpu.VMEM),) * 2,
        scratch_shapes=[
            pltpu.VMEM(flat.shape, BF16),
            pltpu.VMEM((n_act, basis), BF16),
            pltpu.SemaphoreType.DMA((2 * vecs + 1,)),
            pltpu.SemaphoreType.DMA,
        ],
        compiler_params=pltpu.CompilerParams(vmem_limit_bytes=40 * 2**20),
        cost_estimate=pl.CostEstimate(
            flops=2 * vecs * block_rows * basis * 256,
            bytes_accessed=2 * vecs * block_rows * basis,
            transcendentals=0,
        ),
    )(
        orb_pos[None],
        pltpu.with_memory_space_constraint(flat, pltpu.HBM),
        pltpu.with_memory_space_constraint(coeff_t, pltpu.HBM),
    )


def reverse(index, count):
    result = 0
    while count > 1:
        result = 2 * result + index % 2
        index //= 2
        count //= 2
    return result


def chunk_kernel(vecs, half_ref, packed_ref, turned):
    tiles, width, _ = half_ref.shape
    groups = width // SUBLANES
    span = LANES // SUBLANES
    shape = (groups, SUBLANES, LANES)
    row = lax.broadcasted_iota(jnp.int32, shape, 1)
    block = lax.broadcasted_iota(jnp.int32, shape, 2) // span
    source = lax.broadcasted_iota(jnp.int32, (LANES, LANES), 0)
    target = lax.broadcasted_iota(jnp.int32, (LANES, LANES), 1)
    order = jnp.where(source == target % SUBLANES * span + target // SUBLANES, 1.0, 0.0).astype(BF16)
    for tile in range(tiles):
        value = half_ref[tile].reshape(shape)
        for step in (1, 2, 4):
            up = pltpu.roll(pltpu.roll(value, SUBLANES - step, 1), step * span, 2)
            down = pltpu.roll(pltpu.roll(value, step, 1), LANES - step * span, 2)
            swapped = jnp.where(row & step == 0, up, down)
            value = jnp.where((row & step) == (block & step), value, swapped)
        value = jnp.dot(value.reshape(width, LANES).astype(BF16), order, preferred_element_type=F32)
        turned[tile] = value
        per_vec = width // vecs
        half = SUBLANES // 2
        for d in range(2):
            place = reverse(2 * tile + d, 2 * tiles)
            for t in range(per_vec // 2):
                at = t // half * SUBLANES + d * half + t % half
                part = turned[tile, pl.ds(at, vecs, stride=per_vec), :]
                packed_ref[place, :, t * LANES:(t + 1) * LANES] = part.astype(BF16)


def split(half, vecs):
    tiles, width, _ = half.shape
    n_act = width // vecs
    lanes = n_act // 2 * LANES + -(-n_act * n_act // LANES) * LANES
    return pl.pallas_call(
        functools.partial(chunk_kernel, vecs),
        out_shape=jax.ShapeDtypeStruct((2 * tiles, vecs, lanes), BF16),
        in_specs=[pl.BlockSpec(memory_space=pltpu.VMEM)],
        out_specs=pl.BlockSpec(memory_space=pltpu.VMEM),
        scratch_shapes=[pltpu.VMEM(half.shape, F32)],
        compiler_params=pltpu.CompilerParams(vmem_limit_bytes=4 * 2**20),
        cost_estimate=pl.CostEstimate(flops=0, bytes_accessed=2**20, transcendentals=0),
    )(half)


def pack_kernel(vecs, n_act, packed_in, own_ref, other_ref, packed_ref):
    chunks, _, lanes = packed_ref.shape
    first = n_act // 2 * LANES
    total = (own_ref[...] + other_ref[...]).astype(BF16).astype(F32)
    tall = jnp.concatenate([total[:, q * n_act:(q + 1) * n_act] for q in range(vecs)], axis=0)
    shape = (n_act, lanes - first)
    place = lax.broadcasted_iota(jnp.int32, shape, 0)
    lane = lax.broadcasted_iota(jnp.int32, shape, 1)
    spread = jnp.where(lane % n_act == place, 1.0, 0.0).astype(BF16)
    wide = jnp.dot(tall.astype(BF16), spread, preferred_element_type=F32)
    picked = jnp.where(lane // n_act == place, 1.0, 0.0)
    flat = jnp.concatenate(
        [
            jnp.sum(wide[q * n_act:(q + 1) * n_act] * picked, axis=0, keepdims=True)
            for q in range(vecs)
        ],
        axis=0,
    )
    tail = flat.astype(BF16)
    for c in range(chunks):
        packed_ref[c, :, :first] = packed_in[c, :, :first]
        packed_ref[c, :, first:] = tail


def pack(packed, own, other, vecs, n_act):
    return pl.pallas_call(
        functools.partial(pack_kernel, vecs, n_act),
        out_shape=jax.ShapeDtypeStruct(packed.shape, BF16),
        in_specs=[pl.BlockSpec(memory_space=pltpu.VMEM)] * 3,
        out_specs=pl.BlockSpec(memory_space=pltpu.VMEM),
        compiler_params=pltpu.CompilerParams(vmem_limit_bytes=4 * 2**20),
        cost_estimate=pl.CostEstimate(flops=0, bytes_accessed=2**18, transcendentals=0),
    )(packed, own, other)


def finish_kernel(vecs, n_act, moved_ref, density_hbm, out_hbm, fock_ref, wide, left, active, stack, density, folded, weights, out_buf, sems, density_sem):
    sources = moved_ref.shape[0]
    rows_here = LANES // 2
    pairs = n_act * n_act
    total = sources * vecs
    groups = n_act // SUBLANES
    span = LANES // SUBLANES
    parts = rows_here // span
    density_copy = pltpu.make_async_copy(density_hbm, density, density_sem)
    density_copy.start()

    def collect(t):
        for s in range(sources):
            part = moved_ref[s, :, t * LANES:(t + 1) * LANES].astype(F32)
            wide[t, s * vecs:(s + 1) * vecs, :] = part
        return wide[t].astype(BF16)

    for j in range(active.shape[1] // LANES):
        active[:, j * LANES:(j + 1) * LANES] = collect(groups * parts + j)
    def arrange(g):
        for p in range(parts):
            value = collect(g * parts + p)
            cols = slice(p * LANES, (p + 1) * LANES)
            stack[g * total:(g + 1) * total, cols] = value
            left[g, cols] = value.T

    copies = []
    arrange(0)
    for g in range(groups):
        value = jnp.dot(left[g], active[:, :pairs], preferred_element_type=F32)
        if g + 1 < groups:
            arrange(g + 1)
        out_buf[g] = value.reshape(rows_here, SUBLANES, pairs)
        copies.append(
            pltpu.make_async_copy(
                out_buf.at[g], out_hbm.at[:, pl.ds(g * SUBLANES, SUBLANES), :], sems.at[g]
            )
        )
        copies[-1].start()
    density_copy.wait()
    folded[:, :total] = lax.dot_general(
        density[...], active[:, :pairs], (((1,), (1,)), ((), ())), preferred_element_type=F32
    )
    for u in range(n_act):
        value = folded[pl.ds(u, n_act, stride=n_act), :][:, :total]
        high = value.astype(BF16).astype(F32)
        rows = slice(u % SUBLANES * n_act, (u % SUBLANES + 1) * n_act)
        cols = slice(u // SUBLANES * total, (u // SUBLANES + 1) * total)
        weights[0, rows, cols] = high
        weights[1, rows, cols] = value - high
    both = weights[...].reshape(2 * SUBLANES * n_act, groups * total).astype(BF16)
    both = jnp.dot(both, stack[...], preferred_element_type=F32)
    sums = both[:SUBLANES * n_act] + both[SUBLANES * n_act:]
    lane = lax.broadcasted_iota(jnp.int32, (n_act, rows_here * SUBLANES), 1) % SUBLANES
    rest = sums[:n_act]
    for u in range(1, SUBLANES):
        rest = jnp.where(lane == u, sums[u * n_act:(u + 1) * n_act], rest)
    shape = (rows_here * SUBLANES, rows_here)
    member = lax.broadcasted_iota(jnp.int32, shape, 0) // SUBLANES
    member = jnp.where(member == lax.broadcasted_iota(jnp.int32, shape, 1), 1.0, 0.0).astype(BF16)
    result = jnp.zeros((n_act, rows_here), F32)
    for _ in range(2):
        piece = rest.astype(BF16)
        rest = rest - piece.astype(F32)
        result += jnp.dot(piece, member, preferred_element_type=F32)
    fock_ref[...] = result
    for each in copies:
        each.wait()


def finish(moved, density, vecs, n_act):
    sources, _, lanes = moved.shape
    rows_here = LANES // 2
    total = sources * vecs
    pairs = n_act * n_act
    groups = n_act // SUBLANES
    padded = -(-pairs // LANES) * LANES
    return pl.pallas_call(
        functools.partial(finish_kernel, vecs, n_act),
        out_shape=(
            jax.ShapeDtypeStruct((rows_here, n_act, pairs), F32),
            jax.ShapeDtypeStruct((n_act, rows_here), F32),
        ),
        in_specs=[
            pl.BlockSpec(memory_space=pltpu.VMEM),
            pl.BlockSpec(memory_space=pltpu.HBM),
        ],
        out_specs=(pl.BlockSpec(memory_space=pl.ANY), pl.BlockSpec(memory_space=pltpu.VMEM)),
        scratch_shapes=[
            pltpu.VMEM((lanes // LANES, total, LANES), F32),
            pltpu.VMEM((groups, rows_here * SUBLANES, total), BF16),
            pltpu.VMEM((total, padded), BF16),
            pltpu.VMEM((groups * total, rows_here * SUBLANES), BF16),
            pltpu.VMEM((pairs, pairs), BF16),
            pltpu.VMEM((pairs, LANES), F32),
            pltpu.VMEM((2, SUBLANES * n_act, groups * total), F32),
            pltpu.VMEM((groups, rows_here, SUBLANES, pairs), F32),
            pltpu.SemaphoreType.DMA((groups,)),
            pltpu.SemaphoreType.DMA,
        ],
        compiler_params=pltpu.CompilerParams(vmem_limit_bytes=16 * 2**20),
        cost_estimate=pl.CostEstimate(
            flops=2 * rows_here * n_act * total * pairs,
            bytes_accessed=4 * rows_here * n_act * pairs,
            transcendentals=0,
        ),
    )(moved, pltpu.with_memory_space_constraint(density, pltpu.HBM))


def orb_partner(value, step):
    count = lax.axis_size("orb")
    return lax.ppermute(value, "orb", [(i, i ^ step) for i in range(count)])


def exchange_sum(value):
    step = 1
    while step < lax.axis_size("orb"):
        value = value + orb_partner(value, step)
        step *= 2
    return value


def packed_shards(cholesky, active_coeff, pair_density):
    vec_count = lax.axis_size("vec")
    orb_pos = lax.axis_index("orb")
    local_vecs, block_rows, _ = cholesky.shape
    n_act = active_coeff.shape[1]
    pairs = n_act * n_act
    half, partial_value = transform(cholesky, active_coeff.T, orb_pos)
    step = 1
    while 2 * step < lax.axis_size("orb"):
        partial_value = partial_value + orb_partner(partial_value, step)
        step *= 2
    other = orb_partner(partial_value, step)
    packed = pack(split(half, local_vecs), partial_value, other, local_vecs, n_act)
    order = [reverse(i, vec_count) for i in range(vec_count)]
    moved = lax.all_to_all(packed, "vec", 0, 0, axis_index_groups=[order], tiled=True)
    density = pair_density.reshape(pairs, pairs)
    integrals, fock = finish(moved, density, local_vecs, n_act)
    return (integrals, fock.T)


def plain_shards(cholesky, active_coeff, pair_density):
    vec_count = lax.axis_size("vec")
    orb_pos = lax.axis_index("orb")
    local_vecs, block_rows, _ = cholesky.shape
    n_act = active_coeff.shape[1]
    rows_here = block_rows // vec_count
    half = jnp.einsum("qmn,nu->mqu", cholesky, active_coeff, preferred_element_type=F32).astype(BF16)
    coeff_rows = lax.dynamic_slice_in_dim(active_coeff, orb_pos * block_rows, block_rows, 0)
    partial_value = jnp.einsum("mv,mqw->vqw", coeff_rows, half, preferred_element_type=F32)
    own = exchange_sum(partial_value.reshape(n_act, local_vecs * n_act)).astype(BF16)
    flat = half.reshape(vec_count, rows_here, local_vecs * n_act)
    packed = jnp.concatenate([flat, jnp.broadcast_to(own[None], (vec_count,) + own.shape)], axis=1)
    moved = lax.all_to_all(packed, "vec", split_axis=0, concat_axis=0, tiled=True)
    moved = moved.reshape(vec_count, rows_here + n_act, local_vecs, n_act)
    regrouped = moved[:, :rows_here]
    active = moved[:, rows_here:].transpose(0, 2, 1, 3).reshape(vec_count, local_vecs, n_act * n_act)
    integrals = jnp.einsum("smqu,sqx->mux", regrouped, active, preferred_element_type=F32)
    fock = jnp.dot(
        integrals.reshape(rows_here, -1),
        pair_density.astype(F32).reshape(n_act, -1).T,
        precision=lax.Precision.HIGHEST,
    )
    return (integrals, fock)


def shards(cholesky, active_coeff, pair_density):
    vecs, block_rows, basis = cholesky.shape
    n_act = active_coeff.shape[1]
    vec_count = lax.axis_size("vec")
    fits = (
        block_rows == vec_count * (LANES // 2)
        and vec_count % 16 == 0
        and vec_count & (vec_count - 1) == 0
        and lax.axis_size("orb") > 1
        and vecs % 2 == 0
        and vecs * n_act <= LANES
        and vecs * n_act % 16 == 0
        and n_act % SUBLANES == 0
    )
    body = packed_shards if fits else plain_shards
    return body(cholesky, active_coeff, pair_density)


def solution(mesh):
    return jax.shard_map(
        shards,
        mesh=mesh,
        in_specs=(P("vec", "orb", None), P(), P()),
        out_specs=(P(("orb", "vec"), None, None), P(("orb", "vec"), None)),
        check_vma=False,
    )
```
